32 devices in a mesh: group: 2 (over y), wide: 4 (over x, core), narrow: 4 (over z).
Axes of the slice: x: 2, y: 2, z: 4, core: 2. Of those that a mesh axis runs over, the one named last changes fastest.
Arguments:
- query_factor: bfloat16 [4, 128, 1536, 128], P('group', 'narrow', 'wide'), parts along dimension 0, may hold values from -6 to 6
- latent_factor: bfloat16 [4, 128, 512, 128], P('group', 'narrow', 'wide'), parts along dimension 0, may hold values from -6 to 6
- head_owner: int32 [4, 128], P('group'), parts along dimension 0, may hold values from 0 to 3, as said below
Outputs:
- absorbed_owned: bfloat16 [4, 256, 1536, 512], P('group', 'narrow', 'wide'), parts along dimension 0
The draws below stay inside these ranges and needn't reach their ends.
There are 2 independent parts, one for each index of `group`. The reference program is written for one: setup_inputs(seed, part) draws one part's arguments, and reference() takes and returns one part's arrays. A program takes and returns all parts, laid end to end along the dimension named above; each array names one. Nothing has to cross between parts.
Inputs may be any that keep to these rules, and one draw needn't show every extreme that they name: `head_owner`: in each layer, at most 16 of the 32 heads of each aligned block of heads (heads k * 32 to (k + 1) * 32 - 1) have one owner, and some owner takes exactly 16 from every block, so holds 64 heads.
All inputs are finite; a program needn't handle non-finite values.
Results may differ from the reference program's by a relative error of at most 0.001.
Values may be sent and summed in bfloat16 or wider, within the bound.
A program may use at most 192 MiB of HBM per device.

```python
import jax
import jax.numpy as jnp
from jax import lax

H = 128
QL = 1536
KL = 512
HD = 128
LAYERS = 2
HEAD_DEV = 32
SEND = 16
CAP = 64
N_NARROW = 4


def draw_head_owner(key, part):
    key = jax.random.fold_in(key, 11)
    first_key, second_key = jax.random.split(key)
    heavy_owner = jax.random.randint(first_key, (LAYERS,), 0, N_NARROW)
    block_keys = jax.random.split(second_key, LAYERS * N_NARROW)
    heavy_each = jnp.repeat(heavy_owner, N_NARROW)

    def one_block(block_key, heavy_one):
        shuffle_key, spare_key = jax.random.split(block_key)
        spare_slots = jax.random.permutation(spare_key, (N_NARROW - 1) * SEND)[:HEAD_DEV - SEND]
        others = (heavy_one + 1 + spare_slots // SEND) % N_NARROW
        owners = jnp.concatenate([jnp.full((SEND,), heavy_one, jnp.int32), others.astype(jnp.int32)])
        return jax.random.permutation(shuffle_key, owners)
    blocks = jax.vmap(one_block)(block_keys, heavy_each)
    return blocks.reshape(LAYERS, H).astype(jnp.int32)


def steps_of(stream_key, dims, cuts, least, largest):
    factor_of = 1.0
    for dim, parts in cuts:
        steps = jax.random.uniform(jax.random.fold_in(jax.random.fold_in(stream_key, 6), dim), (parts,), jnp.float32, least / len(cuts), largest / len(cuts))
        factor_of = factor_of * jnp.repeat(jnp.exp(steps), dims[dim] // parts).reshape((-1,) + (1,) * (len(dims) - 1 - dim))
    return factor_of


def normal_values(key, shape, deviation, reach, cuts=(), kind=jnp.bfloat16):
    array = deviation * jax.random.normal(key, shape, jnp.float32)
    if cuts:
        array = array * steps_of(key, shape, cuts, -0.22, 0.18)
    return jnp.clip(array, -reach, reach).astype(kind)


def setup_inputs(seed: int = 0, part: int = 0) -> dict:
    seeds = jax.random.split(jax.random.key(seed), 4)
    part_keys = jax.random.split(jax.random.fold_in(seeds[3], part), 4)
    return {
        "query_factor": normal_values(part_keys[0], (LAYERS, H, QL, HD), 1.0, 6.0, ((1, 4), (2, 4))),
        "latent_factor": normal_values(part_keys[1], (LAYERS, H, KL, HD), 1.0, 6.0, ((1, 4), (2, 4))),
        "head_owner": draw_head_owner(jax.random.fold_in(jax.random.fold_in(seeds[3], part), 71), part),
    }


qk_scale = 192.0 ** -0.5


def slot_table(owners):
    onehot = (owners[:, None] == jnp.arange(N_NARROW, dtype=jnp.int32)[None, :]).astype(jnp.int32)
    before = jnp.cumsum(onehot, axis=0) - onehot
    within = jnp.sum(before * onehot, axis=1)
    return (owners * CAP + within).astype(jnp.int32)


def reference(query_factor, latent_factor, head_owner):
    slot_of_head = jax.vmap(slot_table)(head_owner)
    match_table = (slot_of_head[:, :, None] == jnp.arange(N_NARROW * CAP, dtype=jnp.int32)[None, None, :]).astype(jnp.int32)
    source = jnp.sum(match_table * jnp.arange(H, dtype=jnp.int32)[None, :, None], axis=1).astype(jnp.int32)
    filled = jnp.sum(match_table, axis=1) > 0
    layer_ids = jnp.broadcast_to(jnp.arange(LAYERS, dtype=jnp.int32)[:, None], source.shape)

    def one_slot(packed):
        layer_index, source_head, is_live = packed
        query_rows = query_factor[layer_index, source_head].astype(jnp.float32)
        latent_rows = latent_factor[layer_index, source_head].astype(jnp.float32)
        product = jnp.dot(query_rows, latent_rows.T, precision=lax.Precision.HIGHEST) * qk_scale
        return jnp.where(is_live, product, 0.0).astype(jnp.bfloat16)

    result = lax.map(one_slot, (layer_ids.reshape(-1), source.reshape(-1), filled.reshape(-1)))
    return result.reshape(LAYERS, N_NARROW * CAP, QL, KL)
```

```python
import functools

import jax
import jax.numpy as jnp
from jax import lax
from jax.experimental import pallas as pl
from jax.experimental.pallas import tpu as pltpu
from jax.sharding import PartitionSpec as P

qk_scale = 192.0 ** (-0.5)
MESH = pl.DeviceIdType.MESH


def send_rows(local_owner, bucket):
    heads = local_owner.shape[1]
    same = local_owner[:, :, None] == local_owner[:, None, :]
    earlier = jnp.arange(heads)[None, :, None] > jnp.arange(heads)[None, None, :]
    rank = jnp.sum((same & earlier).astype(jnp.int32), axis=2)
    return local_owner * bucket + rank


def slot_sources(head_owner, own_index, peers, bucket):
    layers = head_owner.shape[0]
    counts = jnp.sum((head_owner.reshape(layers, peers, -1) == own_index).astype(jnp.int32), axis=2)
    upto = jnp.arange(peers)[:, None] >= jnp.arange(peers)[None, :]
    ends = jnp.sum(jnp.where(upto[None], counts[:, None, :], 0), axis=2)
    starts = ends - counts
    slots = jnp.arange(peers * bucket, dtype=jnp.int32)[None, :, None]
    held = (slots >= starts[:, None, :]) & (slots < ends[:, None, :])
    rows = jnp.arange(peers, dtype=jnp.int32)[None, None, :] * bucket + slots - starts[:, None, :]
    source = jnp.sum(jnp.where(held, rows, 0), axis=2)
    source = source + (jnp.arange(layers, dtype=jnp.int32) * (peers * bucket))[:, None]
    live = jnp.any(held, axis=2).astype(jnp.int32)
    return source.reshape(-1), live.reshape(-1)


def pack_kernel(rows_ref, query_ref, latent_ref, sent_query_ref, sent_latent_ref, sems):
    layers, heads = query_ref.shape[:2]

    @pl.loop(0, layers * heads)
    def _(i):
        layer, head = i // heads, i % heads
        row = rows_ref[i]
        pltpu.make_async_copy(latent_ref.at[layer, head], sent_latent_ref.at[layer, row], sems.at[0]).start()
        pltpu.make_async_copy(query_ref.at[layer, head], sent_query_ref.at[layer, row], sems.at[1]).start()

    pltpu.make_async_copy(latent_ref, latent_ref, sems.at[0]).wait()
    pltpu.make_async_copy(query_ref, query_ref, sems.at[1]).wait()


def pack(rows, query_factor, latent_factor, width):
    layers = query_factor.shape[0]
    return pl.pallas_call(
        pack_kernel,
        out_shape=(
            jax.ShapeDtypeStruct((layers, width) + query_factor.shape[2:], jnp.bfloat16),
            jax.ShapeDtypeStruct((layers, width) + latent_factor.shape[2:], jnp.bfloat16),
        ),
        grid_spec=pltpu.PrefetchScalarGridSpec(
            num_scalar_prefetch=1,
            grid=(),
            in_specs=[pl.BlockSpec(memory_space=pl.ANY)] * 2,
            out_specs=(pl.BlockSpec(memory_space=pl.ANY),) * 2,
            scratch_shapes=[pltpu.SemaphoreType.DMA((2,))],
        ),
    )(rows.reshape(-1), query_factor, latent_factor)


def exchange_kernel(
    peers, wides, bucket, sent_query_ref, sent_latent_ref, got_query_ref, got_latent_ref,
    query_send, query_recv, latent_send, latent_recv, wide_send, wide_recv, local_sem,
):
    group, wide, me = lax.axis_index("group"), lax.axis_index("wide"), lax.axis_index("narrow")
    layers = sent_query_ref.shape[0]
    part = sent_latent_ref.shape[2]

    def at_narrow(other):
        return (group, wide, other)

    def at_wide(step):
        return (group, lax.rem(wide + step, wides), me)

    barrier = pltpu.get_barrier_semaphore()
    for k in range(1, peers):
        pl.semaphore_signal(barrier, inc=1, device_id=at_narrow(lax.rem(me + k, peers)), device_id_type=MESH)

    @pl.loop(1, wides)
    def _(step):
        pl.semaphore_signal(barrier, inc=1, device_id=at_wide(step), device_id_type=MESH)

    pl.semaphore_wait(barrier, peers - 1 + wides - 1)

    def heads_of(peer):
        return pl.ds(pl.multiple_of(peer * bucket, bucket), bucket)

    def part_of(index):
        return pl.ds(pl.multiple_of(index * part, part), part)

    def narrow_query(layer, k):
        other = lax.rem(me + k, peers)
        return pltpu.make_async_remote_copy(
            src_ref=sent_query_ref.at[layer, heads_of(other)],
            dst_ref=got_query_ref.at[layer, heads_of(me)],
            send_sem=query_send.at[layer, k],
            recv_sem=query_recv.at[layer, k],
            device_id=at_narrow(other),
            device_id_type=MESH,
        )

    def narrow_latent(layer, k):
        other = lax.rem(me + k, peers)
        return pltpu.make_async_remote_copy(
            src_ref=sent_latent_ref.at[layer, heads_of(other)],
            dst_ref=got_latent_ref.at[layer, heads_of(me), part_of(wide)],
            send_sem=latent_send.at[layer, k],
            recv_sem=latent_recv.at[layer, k],
            device_id=at_narrow(other),
            device_id_type=MESH,
        )

    def wide_latent(layer, k, step):
        origin = lax.rem(me + peers - k, peers)
        landed = got_latent_ref.at[layer, heads_of(origin), part_of(wide)]
        return pltpu.make_async_remote_copy(
            src_ref=sent_latent_ref.at[layer, heads_of(me)] if k == 0 else landed,
            dst_ref=landed,
            send_sem=wide_send.at[layer, k, step],
            recv_sem=wide_recv.at[layer, k, step],
            device_id=at_wide(step),
            device_id_type=MESH,
        )

    def own_query(layer):
        return pltpu.make_async_copy(
            sent_query_ref.at[layer, heads_of(me)], got_query_ref.at[layer, heads_of(me)], local_sem.at[0, layer]
        )

    def own_latent(layer):
        return pltpu.make_async_copy(
            sent_latent_ref.at[layer, heads_of(me)],
            got_latent_ref.at[layer, heads_of(me), part_of(wide)],
            local_sem.at[1, layer],
        )

    for layer in range(layers):
        for k in range(1, peers):
            narrow_latent(layer, k).start()
    for layer in range(layers):
        for k in range(1, peers):
            narrow_query(layer, k).start()
    for layer in range(layers):
        own_query(layer).start()
        own_latent(layer).start()
        pl.loop(1, wides)(lambda step: wide_latent(layer, 0, step).start())
    for layer in range(layers):
        for k in range(1, peers):
            narrow_latent(layer, k).wait_recv()
            pl.loop(1, wides)(lambda step: wide_latent(layer, k, step).start())
    for layer in range(layers):
        for k in range(peers):
            pl.loop(1, wides)(lambda step: wide_latent(layer, k, step).wait())
    for layer in range(layers):
        own_query(layer).wait()
        own_latent(layer).wait()
        for k in range(1, peers):
            narrow_latent(layer, k).wait_send()
            narrow_query(layer, k).wait()


def exchange(sent_query, sent_latent, peers, wides, bucket):
    layers, width, part, depth = sent_latent.shape
    dma = pltpu.SemaphoreType.DMA
    return pl.pallas_call(
        functools.partial(exchange_kernel, peers, wides, bucket),
        out_shape=(
            jax.ShapeDtypeStruct(sent_query.shape, jnp.bfloat16),
            jax.ShapeDtypeStruct((layers, width, wides * part, depth), jnp.bfloat16),
        ),
        in_specs=[pl.BlockSpec(memory_space=pl.ANY)] * 2,
        out_specs=(pl.BlockSpec(memory_space=pl.ANY),) * 2,
        scratch_shapes=[
            dma((layers, peers)), dma((layers, peers)),
            dma((layers, peers)), dma((layers, peers)),
            dma((layers, peers, wides)), dma((layers, peers, wides)),
            dma((2, layers)),
        ],
        compiler_params=pltpu.CompilerParams(collective_id=0, has_side_effects=True),
    )(sent_query, sent_latent)


def absorb_kernel(each, source_ref, live_ref, *refs):
    queries, latents, out_ref = refs[:each], refs[each:2 * each], refs[2 * each]
    first = pl.program_id(0) * each
    for b in range(each):
        product = lax.dot_general(
            queries[b][0], latents[b][0], (((1,), (1,)), ((), ())), preferred_element_type=jnp.float32
        )
        taken = live_ref[first + b] > 0
        out_ref[b] = jnp.where(taken, product * qk_scale, 0.0).astype(jnp.bfloat16)


def absorb(source, live, got_query, got_latent):
    layers, width, rows, depth = got_query.shape
    columns = got_latent.shape[2]
    slots = layers * width
    each = 4

    def spec(b, size):
        return pl.BlockSpec((1, size, depth), lambda i, source_ref, live_ref: (source_ref[i * each + b], 0, 0))

    query = got_query.reshape(slots, rows, depth)
    latent = got_latent.reshape(slots, columns, depth)
    result = pl.pallas_call(
        functools.partial(absorb_kernel, each),
        out_shape=jax.ShapeDtypeStruct((slots, rows, columns), jnp.bfloat16),
        grid_spec=pltpu.PrefetchScalarGridSpec(
            num_scalar_prefetch=2,
            grid=(slots // each,),
            in_specs=[spec(b, rows) for b in range(each)] + [spec(b, columns) for b in range(each)],
            out_specs=pl.BlockSpec((each, rows, columns), lambda i, source_ref, live_ref: (i, 0, 0)),
        ),
        compiler_params=pltpu.CompilerParams(vmem_limit_bytes=40 * 1024 * 1024),
    )(source, live, *([query] * each), *([latent] * each))
    return result.reshape(layers, width, rows, columns)


def on_device(query_factor, latent_factor, head_owner):
    peers, wides = lax.axis_size("narrow"), lax.axis_size("wide")
    own_index = lax.axis_index("narrow")
    heads_total = head_owner.shape[1]
    bucket = 2 * heads_total // (peers * peers)
    per_device = query_factor.shape[1]
    local_owner = lax.dynamic_slice_in_dim(head_owner, own_index * per_device, per_device, 1)
    rows = send_rows(local_owner, bucket)
    source, live = slot_sources(head_owner, own_index, peers, bucket)
    sent_query, sent_latent = pack(rows, query_factor, latent_factor, peers * bucket)
    got_query, got_latent = exchange(sent_query, sent_latent, peers, wides, bucket)
    return absorb(source, live, got_query, got_latent)


def solution(mesh):
    in_specs = (
        P("group", "narrow", "wide", None),
        P("group", "narrow", "wide", None),
        P("group", None),
    )
    out_specs = P("group", "narrow", "wide", None)
    return jax.shard_map(
        on_device, mesh=mesh, in_specs=in_specs, out_specs=out_specs, check_vma=False
    )
```

```python
import functools

import jax
import jax.numpy as jnp
from jax import lax
from jax.experimental import pallas as pl
from jax.experimental.pallas import tpu as pltpu
from jax.sharding import PartitionSpec as P

qk_scale = 192.0 ** (-0.5)
MESH = pl.DeviceIdType.MESH


def send_rows(local_owner, bucket):
    heads = local_owner.shape[1]
    same = local_owner[:, :, None] == local_owner[:, None, :]
    earlier = jnp.arange(heads)[None, :, None] > jnp.arange(heads)[None, None, :]
    rank = jnp.sum((same & earlier).astype(jnp.int32), axis=2)
    return local_owner * bucket + rank


def slot_sources(head_owner, own_index, peers, bucket):
    layers = head_owner.shape[0]
    counts = jnp.sum((head_owner.reshape(layers, peers, -1) == own_index).astype(jnp.int32), axis=2)
    upto = jnp.arange(peers)[:, None] >= jnp.arange(peers)[None, :]
    ends = jnp.sum(jnp.where(upto[None], counts[:, None, :], 0), axis=2)
    starts = ends - counts
    slots = jnp.arange(peers * bucket, dtype=jnp.int32)[None, :, None]
    held = (slots >= starts[:, None, :]) & (slots < ends[:, None, :])
    rows = jnp.arange(peers, dtype=jnp.int32)[None, None, :] * bucket + slots - starts[:, None, :]
    source = jnp.sum(jnp.where(held, rows, 0), axis=2)
    source = source + (jnp.arange(layers, dtype=jnp.int32) * (peers * bucket))[:, None]
    live = jnp.any(held, axis=2).astype(jnp.int32)
    return source.reshape(-1), live.reshape(-1)


def pack_kernel(rows_ref, query_ref, latent_ref, sent_query_ref, sent_latent_ref, query_vmem, latent_vmem, in_sems, sems):
    layers, heads = query_ref.shape[:2]
    pieces = 4
    each = heads // pieces

    def read(ref, vmem, which, layer, piece):
        part = pl.ds(piece * each, each)
        return pltpu.make_async_copy(ref.at[layer, part], vmem.at[layer, part], in_sems.at[which, layer, piece])

    for layer in range(layers):
        for piece in range(pieces):
            read(latent_ref, latent_vmem, 0, layer, piece).start()
            read(query_ref, query_vmem, 1, layer, piece).start()
    for layer in range(layers):
        for piece in range(pieces):
            read(latent_ref, latent_vmem, 0, layer, piece).wait()
            read(query_ref, query_vmem, 1, layer, piece).wait()

            @pl.loop(piece * each, (piece + 1) * each)
            def _(head):
                row = rows_ref[layer * heads + head]
                pltpu.make_async_copy(latent_vmem.at[layer, head], sent_latent_ref.at[layer, row], sems.at[0]).start()
                pltpu.make_async_copy(query_vmem.at[layer, head], sent_query_ref.at[layer, row], sems.at[1]).start()

    pltpu.make_async_copy(latent_ref, latent_ref, sems.at[0]).wait()
    pltpu.make_async_copy(query_ref, query_ref, sems.at[1]).wait()


def pack(rows, query_factor, latent_factor, width):
    layers = query_factor.shape[0]
    return pl.pallas_call(
        pack_kernel,
        out_shape=(
            jax.ShapeDtypeStruct((layers, width) + query_factor.shape[2:], jnp.bfloat16),
            jax.ShapeDtypeStruct((layers, width) + latent_factor.shape[2:], jnp.bfloat16),
        ),
        grid_spec=pltpu.PrefetchScalarGridSpec(
            num_scalar_prefetch=1,
            grid=(),
            in_specs=[pl.BlockSpec(memory_space=pl.ANY)] * 2,
            out_specs=(pl.BlockSpec(memory_space=pl.ANY),) * 2,
            scratch_shapes=[
                pltpu.VMEM(query_factor.shape, jnp.bfloat16),
                pltpu.VMEM(latent_factor.shape, jnp.bfloat16),
                pltpu.SemaphoreType.DMA((2, layers, 4)),
                pltpu.SemaphoreType.DMA((2,)),
            ],
        ),
        compiler_params=pltpu.CompilerParams(vmem_limit_bytes=40 * 1024 * 1024),
    )(rows.reshape(-1), query_factor, latent_factor)


def exchange_kernel(
    peers, wides, bucket, sent_query_ref, sent_latent_ref, got_query_ref, got_latent_ref,
    query_send, query_recv, latent_send, latent_recv, wide_send, wide_recv, local_sem,
):
    group, wide, me = lax.axis_index("group"), lax.axis_index("wide"), lax.axis_index("narrow")
    layers = sent_query_ref.shape[0]
    part = sent_latent_ref.shape[2]

    def at_narrow(other):
        return (group, wide, other)

    def at_wide(step):
        return (group, lax.rem(wide + step, wides), me)

    barrier = pltpu.get_barrier_semaphore()
    for k in range(1, peers):
        pl.semaphore_signal(barrier, inc=1, device_id=at_narrow(lax.rem(me + k, peers)), device_id_type=MESH)

    @pl.loop(1, wides)
    def _(step):
        pl.semaphore_signal(barrier, inc=1, device_id=at_wide(step), device_id_type=MESH)

    pl.semaphore_wait(barrier, peers - 1 + wides - 1)

    def heads_of(peer):
        return pl.ds(pl.multiple_of(peer * bucket, bucket), bucket)

    def part_of(index):
        return pl.ds(pl.multiple_of(index * part, part), part)

    def narrow_query(layer, k):
        other = lax.rem(me + k, peers)
        return pltpu.make_async_remote_copy(
            src_ref=sent_query_ref.at[layer, heads_of(other)],
            dst_ref=got_query_ref.at[layer, heads_of(me)],
            send_sem=query_send.at[layer, k],
            recv_sem=query_recv.at[layer, k],
            device_id=at_narrow(other),
            device_id_type=MESH,
        )

    def narrow_latent(layer, k):
        other = lax.rem(me + k, peers)
        return pltpu.make_async_remote_copy(
            src_ref=sent_latent_ref.at[layer, heads_of(other)],
            dst_ref=got_latent_ref.at[layer, heads_of(me), part_of(wide)],
            send_sem=latent_send.at[layer, k],
            recv_sem=latent_recv.at[layer, k],
            device_id=at_narrow(other),
            device_id_type=MESH,
        )

    def wide_latent(layer, k, step):
        origin = lax.rem(me + peers - k, peers)
        landed = got_latent_ref.at[layer, heads_of(origin), part_of(wide)]
        return pltpu.make_async_remote_copy(
            src_ref=sent_latent_ref.at[layer, heads_of(me)] if k == 0 else landed,
            dst_ref=landed,
            send_sem=wide_send.at[layer, k, step],
            recv_sem=wide_recv.at[layer, k, step],
            device_id=at_wide(step),
            device_id_type=MESH,
        )

    def own_query(layer):
        return pltpu.make_async_copy(
            sent_query_ref.at[layer, heads_of(me)], got_query_ref.at[layer, heads_of(me)], local_sem.at[0, layer]
        )

    def own_latent(layer):
        return pltpu.make_async_copy(
            sent_latent_ref.at[layer, heads_of(me)],
            got_latent_ref.at[layer, heads_of(me), part_of(wide)],
            local_sem.at[1, layer],
        )

    for layer in range(layers):
        for k in range(1, peers):
            narrow_latent(layer, k).start()
    for layer in range(layers):
        for k in range(1, peers):
            narrow_query(layer, k).start()
    for layer in range(layers):
        own_query(layer).start()
        own_latent(layer).start()
        pl.loop(1, wides)(lambda step: wide_latent(layer, 0, step).start())
    for layer in range(layers):
        for k in range(1, peers):
            narrow_latent(layer, k).wait_recv()
            pl.loop(1, wides)(lambda step: wide_latent(layer, k, step).start())
    for layer in range(layers):
        for k in range(peers):
            pl.loop(1, wides)(lambda step: wide_latent(layer, k, step).wait())
    for layer in range(layers):
        own_query(layer).wait()
        own_latent(layer).wait()
        for k in range(1, peers):
            narrow_latent(layer, k).wait_send()
            narrow_query(layer, k).wait()


def exchange(sent_query, sent_latent, peers, wides, bucket):
    layers, width, part, depth = sent_latent.shape
    dma = pltpu.SemaphoreType.DMA
    return pl.pallas_call(
        functools.partial(exchange_kernel, peers, wides, bucket),
        out_shape=(
            jax.ShapeDtypeStruct(sent_query.shape, jnp.bfloat16),
            jax.ShapeDtypeStruct((layers, width, wides * part, depth), jnp.bfloat16),
        ),
        in_specs=[pl.BlockSpec(memory_space=pl.ANY)] * 2,
        out_specs=(pl.BlockSpec(memory_space=pl.ANY),) * 2,
        scratch_shapes=[
            dma((layers, peers)), dma((layers, peers)),
            dma((layers, peers)), dma((layers, peers)),
            dma((layers, peers, wides)), dma((layers, peers, wides)),
            dma((2, layers)),
        ],
        compiler_params=pltpu.CompilerParams(collective_id=0, has_side_effects=True),
    )(sent_query, sent_latent)


def absorb_kernel(each, source_ref, live_ref, *refs):
    queries, latents, out_ref = refs[:each], refs[each:2 * each], refs[2 * each]
    first = pl.program_id(0) * each
    for b in range(each):
        product = lax.dot_general(
            queries[b][0], latents[b][0], (((1,), (1,)), ((), ())), preferred_element_type=jnp.float32
        )
        taken = live_ref[first + b] > 0
        out_ref[b] = jnp.where(taken, product * qk_scale, 0.0).astype(jnp.bfloat16)


def absorb(source, live, got_query, got_latent):
    layers, width, rows, depth = got_query.shape
    columns = got_latent.shape[2]
    slots = layers * width
    each = 8

    def spec(b, size):
        return pl.BlockSpec((1, size, depth), lambda i, source_ref, live_ref: (source_ref[i * each + b], 0, 0))

    query = got_query.reshape(slots, rows, depth)
    latent = got_latent.reshape(slots, columns, depth)
    result = pl.pallas_call(
        functools.partial(absorb_kernel, each),
        out_shape=jax.ShapeDtypeStruct((slots, rows, columns), jnp.bfloat16),
        grid_spec=pltpu.PrefetchScalarGridSpec(
            num_scalar_prefetch=2,
            grid=(slots // each,),
            in_specs=[spec(b, rows) for b in range(each)] + [spec(b, columns) for b in range(each)],
            out_specs=pl.BlockSpec((each, rows, columns), lambda i, source_ref, live_ref: (i, 0, 0)),
        ),
        compiler_params=pltpu.CompilerParams(vmem_limit_bytes=40 * 1024 * 1024),
    )(source, live, *([query] * each), *([latent] * each))
    return result.reshape(layers, width, rows, columns)


def on_device(query_factor, latent_factor, head_owner):
    peers, wides = lax.axis_size("narrow"), lax.axis_size("wide")
    own_index = lax.axis_index("narrow")
    heads_total = head_owner.shape[1]
    bucket = 2 * heads_total // (peers * peers)
    per_device = query_factor.shape[1]
    local_owner = lax.dynamic_slice_in_dim(head_owner, own_index * per_device, per_device, 1)
    rows = send_rows(local_owner, bucket)
    source, live = slot_sources(head_owner, own_index, peers, bucket)
    sent_query, sent_latent = pack(rows, query_factor, latent_factor, peers * bucket)
    got_query, got_latent = exchange(sent_query, sent_latent, peers, wides, bucket)
    return absorb(source, live, got_query, got_latent)


def solution(mesh):
    in_specs = (
        P("group", "narrow", "wide", None),
        P("group", "narrow", "wide", None),
        P("group", None),
    )
    out_specs = P("group", "narrow", "wide", None)
    return jax.shard_map(
        on_device, mesh=mesh, in_specs=in_specs, out_specs=out_specs, check_vma=False
    )
```

```python
import functools

import jax
import jax.numpy as jnp
from jax import lax
from jax.experimental import pallas as pl
from jax.experimental.pallas import tpu as pltpu
from jax.sharding import PartitionSpec as P

qk_scale = 192.0 ** (-0.5)
MESH = pl.DeviceIdType.MESH


def send_rows(local_owner, bucket):
    heads = local_owner.shape[1]
    same = local_owner[:, :, None] == local_owner[:, None, :]
    earlier = jnp.arange(heads)[None, :, None] > jnp.arange(heads)[None, None, :]
    rank = jnp.sum((same & earlier).astype(jnp.int32), axis=2)
    return local_owner * bucket + rank


def slot_sources(head_owner, own_index, peers, bucket):
    layers = head_owner.shape[0]
    counts = jnp.sum((head_owner.reshape(layers, peers, -1) == own_index).astype(jnp.int32), axis=2)
    upto = jnp.arange(peers)[:, None] >= jnp.arange(peers)[None, :]
    ends = jnp.sum(jnp.where(upto[None], counts[:, None, :], 0), axis=2)
    starts = ends - counts
    slots = jnp.arange(peers * bucket, dtype=jnp.int32)[None, :, None]
    held = (slots >= starts[:, None, :]) & (slots < ends[:, None, :])
    rows = jnp.arange(peers, dtype=jnp.int32)[None, None, :] * bucket + slots - starts[:, None, :]
    source = jnp.sum(jnp.where(held, rows, 0), axis=2)
    live = jnp.any(held, axis=2).astype(jnp.int32)
    return source.reshape(-1), live.reshape(-1)


def pack_kernel(rows_ref, query_ref, latent_ref, *refs):
    layers, heads = query_ref.shape[:2]
    sent_query_refs, sent_latent_refs = refs[:layers], refs[layers:2 * layers]
    query_vmem, latent_vmem, in_sems, sems = refs[2 * layers:]
    pieces = 4
    each = heads // pieces

    def read(ref, vmem, which, layer, piece):
        part = pl.ds(piece * each, each)
        return pltpu.make_async_copy(ref.at[layer, part], vmem.at[layer, part], in_sems.at[which, layer, piece])

    for layer in range(layers):
        for piece in range(pieces):
            read(latent_ref, latent_vmem, 0, layer, piece).start()
            read(query_ref, query_vmem, 1, layer, piece).start()
    for layer in range(layers):
        for piece in range(pieces):
            read(latent_ref, latent_vmem, 0, layer, piece).wait()
            read(query_ref, query_vmem, 1, layer, piece).wait()

            @pl.loop(piece * each, (piece + 1) * each)
            def _(head):
                row = rows_ref[layer * heads + head]
                pltpu.make_async_copy(latent_vmem.at[layer, head], sent_latent_refs[layer].at[row], sems.at[0]).start()
                pltpu.make_async_copy(query_vmem.at[layer, head], sent_query_refs[layer].at[row], sems.at[1]).start()

    pltpu.make_async_copy(latent_ref, latent_ref, sems.at[0]).wait()
    pltpu.make_async_copy(query_ref, query_ref, sems.at[1]).wait()


def pack(rows, query_factor, latent_factor, width):
    layers = query_factor.shape[0]
    query = jax.ShapeDtypeStruct((width,) + query_factor.shape[2:], jnp.bfloat16)
    latent = jax.ShapeDtypeStruct((width,) + latent_factor.shape[2:], jnp.bfloat16)
    sent = pl.pallas_call(
        pack_kernel,
        out_shape=(query,) * layers + (latent,) * layers,
        grid_spec=pltpu.PrefetchScalarGridSpec(
            num_scalar_prefetch=1,
            grid=(),
            in_specs=[pl.BlockSpec(memory_space=pl.ANY)] * 2,
            out_specs=(pl.BlockSpec(memory_space=pl.ANY),) * (2 * layers),
            scratch_shapes=[
                pltpu.VMEM(query_factor.shape, jnp.bfloat16),
                pltpu.VMEM(latent_factor.shape, jnp.bfloat16),
                pltpu.SemaphoreType.DMA((2, layers, 4)),
                pltpu.SemaphoreType.DMA((2,)),
            ],
        ),
        compiler_params=pltpu.CompilerParams(vmem_limit_bytes=56 * 1024 * 1024),
    )(rows.reshape(-1), query_factor, latent_factor)
    return sent[:layers], sent[layers:]


def flow_limits(peers, bucket, heavy):
    half = peers // 2
    limits = [[5 * bucket // 8] * peers for _ in range(peers)]
    for source in range(peers):
        for owner in range(peers):
            if owner == heavy or owner == source:
                limits[source][owner] = bucket
            elif source // half != heavy // half and owner // half == heavy // half:
                limits[source][owner] = bucket // 2
    return limits


def exchange_kernel(
    peers, wides, bucket, plan, sent_query_ref, sent_latent_ref, got_query_ref, got_latent_ref,
    query_send, query_recv, latent_send, latent_recv, wide_send, wide_recv, local_sem,
):
    group, wide, me = lax.axis_index("group"), lax.axis_index("wide"), lax.axis_index("narrow")
    part = sent_latent_ref.shape[1]
    half = peers // 2

    def at_narrow(other):
        return (group, wide, other)

    def at_wide(step):
        return (group, lax.rem(wide + step, wides), me)

    barrier = pltpu.get_barrier_semaphore()
    for k in range(1, peers):
        pl.semaphore_signal(barrier, inc=1, device_id=at_narrow(lax.rem(me + k, peers)), device_id_type=MESH)

    @pl.loop(1, wides)
    def _(step):
        pl.semaphore_signal(barrier, inc=1, device_id=at_wide(step), device_id_type=MESH)

    pl.semaphore_wait(barrier, peers - 1 + wides - 1)

    def for_size(source, owner, act):
        if plan is None:
            act(bucket)
            return
        heavy = plan[0]
        for index in range(1, len(plan)):
            heavy = heavy + (plan[index] - plan[index - 1]) * (group >= index).astype(jnp.int32)
        hot = owner == heavy
        far = (source // half != heavy // half) & (owner // half == heavy // half)
        pl.when(hot)(lambda: act(bucket))
        pl.when(jnp.logical_not(hot) & far)(lambda: act(bucket // 2))
        pl.when(jnp.logical_not(hot) & jnp.logical_not(far))(lambda: act(5 * bucket // 8))

    def heads_of(peer, size):
        return pl.ds(peer * bucket, size)

    def part_of(index):
        return pl.ds(pl.multiple_of(index * part, part), part)

    def later(k):
        return lax.rem(me + k, peers)

    def earlier(k):
        return lax.rem(me + peers - k, peers)

    def narrow_query(k, size):
        return pltpu.make_async_remote_copy(
            src_ref=sent_query_ref.at[heads_of(later(k), size)],
            dst_ref=got_query_ref.at[heads_of(me, size)],
            send_sem=query_send.at[k],
            recv_sem=query_recv.at[k],
            device_id=at_narrow(later(k)),
            device_id_type=MESH,
        )

    def narrow_latent(k, size):
        return pltpu.make_async_remote_copy(
            src_ref=sent_latent_ref.at[heads_of(later(k), size)],
            dst_ref=got_latent_ref.at[heads_of(me, size), part_of(wide)],
            send_sem=latent_send.at[k],
            recv_sem=latent_recv.at[k],
            device_id=at_narrow(later(k)),
            device_id_type=MESH,
        )

    def wide_latent(k, step, size):
        landed = got_latent_ref.at[heads_of(earlier(k), size), part_of(wide)]
        return pltpu.make_async_remote_copy(
            src_ref=sent_latent_ref.at[heads_of(me, size)] if k == 0 else landed,
            dst_ref=landed,
            send_sem=wide_send.at[k, step],
            recv_sem=wide_recv.at[k, step],
            device_id=at_wide(step),
            device_id_type=MESH,
        )

    def all_wide(k, act):
        return lambda size: pl.loop(1, wides)(lambda step: act(wide_latent(k, step, size)))

    own_query = pltpu.make_async_copy(
        sent_query_ref.at[heads_of(me, bucket)], got_query_ref.at[heads_of(me, bucket)], local_sem.at[0]
    )
    own_latent = pltpu.make_async_copy(
        sent_latent_ref.at[heads_of(me, bucket)], got_latent_ref.at[heads_of(me, bucket), part_of(wide)], local_sem.at[1]
    )

    for k in range(1, peers):
        for_size(me, later(k), lambda size: narrow_latent(k, size).start())
    for k in range(1, peers):
        for_size(me, later(k), lambda size: narrow_query(k, size).start())
    own_query.start()
    own_latent.start()
    all_wide(0, lambda copy: copy.start())(bucket)
    for k in range(1, peers):
        for_size(earlier(k), me, lambda size: narrow_latent(k, size).wait_recv())
        for_size(earlier(k), me, all_wide(k, lambda copy: copy.start()))
    all_wide(0, lambda copy: copy.wait())(bucket)
    for k in range(1, peers):
        for_size(earlier(k), me, all_wide(k, lambda copy: copy.wait()))
    own_query.wait()
    own_latent.wait()
    for k in range(1, peers):
        for_size(me, later(k), lambda size: narrow_latent(k, size).wait_send())
        for_size(me, later(k), lambda size: narrow_query(k, size).wait_send())
        for_size(earlier(k), me, lambda size: narrow_query(k, size).wait_recv())


def exchange(peers, wides, bucket, plan, collective_id, sent_query, sent_latent):
    width, part, depth = sent_latent.shape
    dma = pltpu.SemaphoreType.DMA
    return pl.pallas_call(
        functools.partial(exchange_kernel, peers, wides, bucket, plan),
        out_shape=(
            jax.ShapeDtypeStruct(sent_query.shape, jnp.bfloat16),
            jax.ShapeDtypeStruct((width, wides * part, depth), jnp.bfloat16),
        ),
        in_specs=[pl.BlockSpec(memory_space=pl.ANY)] * 2,
        out_specs=(pl.BlockSpec(memory_space=pl.ANY),) * 2,
        scratch_shapes=[
            dma((peers,)), dma((peers,)), dma((peers,)), dma((peers,)),
            dma((peers, wides)), dma((peers, wides)), dma((2,)),
        ],
        compiler_params=pltpu.CompilerParams(collective_id=collective_id, has_side_effects=True),
    )(sent_query, sent_latent)


def choose_plans(head_owner, peers, bucket, groups):
    layers = head_owner.shape[0]
    owners = jnp.arange(peers, dtype=jnp.int32)
    blocks = head_owner.reshape(layers, peers, -1)
    counts = jnp.sum((blocks[:, :, :, None] == owners).astype(jnp.int32), axis=2)
    limits = jnp.array([flow_limits(peers, bucket, heavy) for heavy in range(peers)], jnp.int32)
    fits = jnp.all(counts[:, None] <= limits[None], axis=(2, 3))
    heavy = jnp.min(jnp.where(fits, owners[None], peers), axis=1)
    digit = jnp.where(heavy < peers, heavy, 0)
    for index in range(1, groups):
        digit = jnp.where(lax.axis_index("group") >= index, digit * peers, digit)
    plans = peers ** groups
    return jnp.minimum(lax.psum(jnp.where(heavy < peers, digit, plans), "group"), plans)


def absorb_kernel(layers, each, source_ref, live_ref, *refs):
    out_ref = refs[2 * layers * each]
    step = pl.program_id(0)
    steps = pl.num_programs(0) // layers
    for layer in range(layers):

        @pl.when(step // steps == layer)
        def _():
            queries = refs[layer * each:(layer + 1) * each]
            latents = refs[(layers + layer) * each:(layers + layer + 1) * each]
            for b in range(each):
                product = lax.dot_general(
                    queries[b][0], latents[b][0], (((1,), (1,)), ((), ())), preferred_element_type=jnp.float32
                )
                taken = live_ref[step * each + b] > 0
                out_ref[b] = jnp.where(taken, product * qk_scale, 0.0).astype(jnp.bfloat16)


def absorb(source, live, queries, latents):
    layers = len(queries)
    width, rows, depth = queries[0].shape
    columns = latents[0].shape[1]
    slots = layers * width
    each = 8
    steps = width // each

    def spec(layer, b, size):
        def block(i, source_ref, live_ref):
            step = jnp.clip(i, layer * steps, (layer + 1) * steps - 1)
            return (source_ref[step * each + b], 0, 0)

        return pl.BlockSpec((1, size, depth), block)

    result = pl.pallas_call(
        functools.partial(absorb_kernel, layers, each),
        out_shape=jax.ShapeDtypeStruct((slots, rows, columns), jnp.bfloat16),
        grid_spec=pltpu.PrefetchScalarGridSpec(
            num_scalar_prefetch=2,
            grid=(layers * steps,),
            in_specs=[spec(layer, b, size) for size in (rows, columns) for layer in range(layers) for b in range(each)],
            out_specs=pl.BlockSpec((each, rows, columns), lambda i, source_ref, live_ref: (i, 0, 0)),
        ),
        compiler_params=pltpu.CompilerParams(vmem_limit_bytes=56 * 1024 * 1024),
    )(source, live, *[array for arrays in (queries, latents) for array in arrays for _ in range(each)])
    return result.reshape(layers, width, rows, columns)


def on_device(query_factor, latent_factor, head_owner):
    peers, wides, groups = lax.axis_size("narrow"), lax.axis_size("wide"), lax.axis_size("group")
    own_index = lax.axis_index("narrow")
    layers, heads_total = head_owner.shape
    bucket = 2 * heads_total // (peers * peers)
    per_device = query_factor.shape[1]
    local_owner = lax.dynamic_slice_in_dim(head_owner, own_index * per_device, per_device, 1)
    rows = send_rows(local_owner, bucket)
    source, live = slot_sources(head_owner, own_index, peers, bucket)
    sent_queries, sent_latents = pack(rows, query_factor, latent_factor, peers * bucket)
    plans = peers ** groups
    full = functools.partial(exchange, peers, wides, bucket, None, 0)
    if plans > 16 or bucket % 8:
        exchanges = [full(*sent) for sent in zip(sent_queries, sent_latents)]
    else:
        chosen = choose_plans(head_owner, peers, bucket, groups)
        branches = []
        for number in range(plans):
            plan = tuple(number // peers ** index % peers for index in range(groups))
            branches.append(functools.partial(exchange, peers, wides, bucket, plan, number + 1))
        branches.append(full)
        exchanges = [
            lax.switch(chosen[layer], branches, sent_queries[layer], sent_latents[layer]) for layer in range(layers)
        ]
    queries, latents = zip(*exchanges)
    return absorb(source, live, queries, latents)


def solution(mesh):
    in_specs = (
        P("group", "narrow", "wide", None),
        P("group", "narrow", "wide", None),
        P("group", None),
    )
    out_specs = P("group", "narrow", "wide", None)
    return jax.shard_map(
        on_device, mesh=mesh, in_specs=in_specs, out_specs=out_specs, check_vma=False
    )
```
